32 devices in a mesh: tensor: 4 (over y, core), store: 8 (over z, x).
Axes of the slice: x: 2, y: 2, z: 4, core: 2. Of those that a mesh axis runs over, the one named last changes fastest.
Arguments:
- inputs: bfloat16 [256, 16, 28672], P('tensor', None, 'store'), may hold values from -6 to 6
- out_grads: bfloat16 [256, 16, 8192], P('tensor', None, 'store'), may hold values from -6 to 6
- proj_in: bfloat16 [28672, 128], P('store'), may hold values from -0.03125 to 0.03125
- proj_out: bfloat16 [8192, 128], P('store'), may hold values from -0.09375 to 0.09375
- inv_fisher: float32 [16384, 16384], P('store', 'tensor'), may hold values from -1 to 4
- store_grads: float32 [2048, 16384], P('store', 'tensor'), may hold values from -0.005859375 to 0.005859375
Outputs:
- scores: float32 [256, 2048], P('tensor', 'store')
The draws below stay inside these ranges and needn't reach their ends.
All inputs are finite; a program needn't handle non-finite values.
Results may differ from the reference program's by a relative error of at most 0.0003.
Values sent between devices are 32-bit elements; how exact they have to be, the bound alone decides.
A program may use at most 128 MiB of HBM per device.

```python
import math
import jax
import jax.numpy as jnp
from jax import lax

IN = 28672
OUT = 8192
PJ = 128
PK = 128
TOK = 16
EXAMPLES = 256
STORED = 2048
COORDS = 16384


def draw_inv_fisher(key, part):
    key_off = jax.random.fold_in(key, 11)
    key_diag = jax.random.fold_in(key, 12)
    coords = PK * PJ
    off_diag = jax.random.uniform(key_off, (coords, coords), jnp.float32, -0.9, 0.9)
    off_diag = off_diag / math.sqrt(coords)
    diag_values = 1.0 + 2.0 * jax.random.uniform(key_diag, (coords,), jnp.float32)
    positions = jnp.arange(coords)
    return off_diag.at[positions, positions].add(diag_values)


def with_spikes(array, own_key, source, target, shards_of, factor):
    owner, partner = [(jnp.arange(array.shape[axis_at]) // (array.shape[axis_at] // shards_of)).reshape([-1 if axis == axis_at else 1 for axis in range(array.ndim)]) for axis_at in (source, target)]
    chosen = jax.random.permutation(own_key, shards_of)[partner]
    strong = (owner == chosen) | (owner == (partner + shards_of // 2) % shards_of)
    return jnp.where(strong, factor * array, array)


def block_levels(stream_key, extent, cuts, least, largest):
    def one(axis_at, blocks):
        draws = jax.random.uniform(jax.random.fold_in(jax.random.fold_in(stream_key, 6), axis_at), (blocks,), jnp.float32, least / len(cuts), largest / len(cuts))
        return jnp.repeat(jnp.exp(draws), extent[axis_at] // blocks).reshape((-1,) + (1,) * (len(extent) - axis_at - 1))

    loudness = one(*cuts[0])
    for cut in cuts[1:]:
        loudness = loudness * one(*cut)
    return loudness


def scatter_about(rng, extent, deviation, reach, cuts=(), held_as=jnp.bfloat16):
    drawn = deviation * jax.random.normal(rng, extent, jnp.float32)
    if cuts:
        drawn = drawn * block_levels(rng, extent, cuts, -0.22, 0.18)
    return jnp.clip(drawn, -reach, reach).astype(held_as)


def bell_draw_with(rng, shape, scale, reach, cuts, heavy, dtype=jnp.bfloat16):
    drawn = scale * jax.random.normal(rng, shape, jnp.float32)
    if cuts:
        drawn = drawn * block_levels(rng, shape, cuts, -0.22, 0.18)
    return jnp.clip(with_spikes(drawn, jax.random.fold_in(rng, 3), *heavy), -reach, reach).astype(dtype)


def setup_inputs(seed: int = 0) -> dict:
    key_list = jax.random.split(jax.random.key(seed), 7)
    return {
        "inputs": scatter_about(key_list[0], (EXAMPLES, TOK, IN), 1.0, 6.0, ((0, 4), (2, 8))),
        "out_grads": scatter_about(key_list[1], (EXAMPLES, TOK, OUT), 1.0, 6.0, ((0, 4), (2, 8))),
        "proj_in": scatter_about(key_list[2], (IN, PJ), IN ** -0.5, 0.03125, ((0, 8),)),
        "proj_out": bell_draw_with(key_list[3], (OUT, PK), OUT ** -0.5, 0.09375, ((0, 8),), (0, 1, 8, 2.0)),
        "inv_fisher": draw_inv_fisher(jax.random.fold_in(key_list[6], 71), 0),
        "store_grads": scatter_about(key_list[5], (STORED, COORDS), (64 * COORDS) ** -0.5, 0.005859375, ((0, 8), (1, 4)), jnp.float32),
    }


def reference(inputs, out_grads, proj_in, proj_out, inv_fisher, store_grads):
    act_proj = jnp.dot(inputs.reshape(EXAMPLES * TOK, IN), proj_in, preferred_element_type=jnp.float32).reshape(EXAMPLES, TOK, PJ)
    grad_proj = jnp.dot(out_grads.reshape(EXAMPLES * TOK, OUT), proj_out, preferred_element_type=jnp.float32).reshape(EXAMPLES, TOK, PK)
    joined = jnp.einsum("etk,etj->ekj", grad_proj.astype(jnp.float32), act_proj.astype(jnp.float32), precision=lax.Precision.HIGHEST)
    example_grads = joined.reshape(EXAMPLES, PK * PJ)
    preconditioned = jnp.dot(example_grads, inv_fisher, precision=lax.Precision.HIGHEST, preferred_element_type=jnp.float32)
    scores = lax.dot_general(preconditioned, store_grads, (((1,), (1,)), ((), ())), precision=lax.Precision.HIGHEST, preferred_element_type=jnp.float32)
    return scores
```

```python
import functools
import jax
import jax.numpy as jnp
from jax import lax
from jax.experimental import pallas as pl
from jax.experimental.pallas import tpu as pltpu
from jax.sharding import PartitionSpec as P

F32 = jnp.float32
BF16 = jnp.bfloat16
MESH = pl.DeviceIdType.MESH
CORES = 2
LAGS = (0, 2, 3, 4, 5)
SLOTS = 4


def halves(value):
    high = value.astype(BF16)
    low = (value - high.astype(F32)).astype(BF16)
    return high, low


def dot3(left, right, dims):
    lh, ll = left
    rh, rl = right
    dot = functools.partial(
        lax.dot_general, dimension_numbers=(dims, ((), ())), preferred_element_type=F32
    )
    return dot(lh, rh) + (dot(lh, rl) + dot(ll, rh))


def kernel(
    cfg,
    x_hbm, g_hbm, pin_hbm, pout_hbm, f_hbm, s_hbm, out_ref,
    xin, gin, pin, pout, fbuf, sbuf,
    a_part, a_xrecv, a_xred, a_zrecv, a_full, gt,
    e_all, e_hi, e_lo,
    b_part, b_xrecv, b_xred, b_zrecv, b_full,
    score, srecv,
    in_sem, proj_sem, f_sem, s_sem,
    xs_send, xs_recv, zs_send, zs_recv, zg_send, zg_recv, xg_send, xg_recv,
    ey_send, ey_recv, ec_send, ec_recv, sc_send, sc_recv,
):
    X, Z, T, Y = cfg["X"], cfg["Z"], cfg["T"], cfg["Y"]
    NA, NB, TA, CW, TOK = cfg["NA"], cfg["NB"], cfg["TA"], cfg["CW"], cfg["TOK"]
    S = X * Z
    store, tensor = lax.axis_index("store"), lax.axis_index("tensor")
    mx, mz = lax.rem(store, X), store // X
    my, mc = tensor // CORES, lax.rem(tensor, CORES)
    pj = pin.shape[1]
    pk = pout.shape[1]
    ks = pk // S
    ex_here = xin.shape[0] // TOK
    ex_all = e_all.shape[0]
    ex_chunk = TA // TOK

    def xpeer(d):
        return lax.rem(mx + d, X)

    def zpeer(d):
        return lax.rem(mz + d, Z)

    def to_x(d):
        return {"store": mz * X + xpeer(d), "tensor": tensor}

    def to_z(d):
        return {"store": zpeer(d) * X + mx, "tensor": tensor}

    def to_t(t):
        return {"store": store, "tensor": t}

    def remote(src, dst, send, recv, device):
        return pltpu.make_async_remote_copy(
            src_ref=src, dst_ref=dst, send_sem=send, recv_sem=recv,
            device_id=device, device_id_type=MESH,
        )

    loads = []
    for c in range(NA):
        rows = pl.ds(c * TA, TA)
        loads.append((
            pltpu.make_async_copy(x_hbm.at[rows], xin.at[rows], in_sem.at[c, 0]),
            pltpu.make_async_copy(g_hbm.at[rows], gin.at[rows], in_sem.at[c, 1]),
        ))
    pin_load = pltpu.make_async_copy(pin_hbm, pin, proj_sem.at[0])
    pout_load = pltpu.make_async_copy(pout_hbm, pout, proj_sem.at[1])
    s_load = pltpu.make_async_copy(s_hbm, sbuf, s_sem.at[0])
    pin_load.start()
    pout_load.start()
    for pair in loads:
        pair[0].start()
        pair[1].start()

    def f_load(q):
        slot = q % SLOTS
        return pltpu.make_async_copy(
            f_hbm.at[:, pl.ds(q * CW, CW)], fbuf.at[slot], f_sem.at[slot]
        )

    for q in range(min(SLOTS, NB)):
        f_load(q).start()
    s_load.start()

    barrier = pltpu.get_barrier_semaphore()
    for d in range(1, X):
        pl.semaphore_signal(barrier, inc=1, device_id=to_x(d), device_id_type=MESH)
    for d in range(1, Z):
        pl.semaphore_signal(barrier, inc=1, device_id=to_z(d), device_id_type=MESH)
    for d in range(1, T):
        pl.semaphore_signal(
            barrier, inc=1, device_id=to_t(lax.rem(tensor + d, T)), device_id_type=MESH
        )
    pl.semaphore_wait(barrier, X + Z + T - 3)

    pending = []

    def begin(copy):
        copy.start()
        pending.append(copy)

    def reducer(base, part, xrecv, xred, zrecv, full):
        rows = part.shape[1]
        rx, rz = rows // X, rows // S

        def at_x(p):
            return pl.ds(pl.multiple_of(p * rx, rx), rx)

        def at_z(p):
            return pl.ds(pl.multiple_of(p * rz, rz), rz)

        def at_own(x, z):
            return pl.ds(pl.multiple_of(x * rx + z * rz, rz), rz)

        def x_copy(q, d):
            return remote(part.at[q, at_x(xpeer(d))], xrecv.at[q, d - 1],
                          xs_send.at[base + q, d - 1], xs_recv.at[base + q, d - 1], to_x(d))

        def z_copy(q, d):
            return remote(xred.at[q, at_z(zpeer(d))], zrecv.at[q, d - 1],
                          zs_send.at[base + q, d - 1], zs_recv.at[base + q, d - 1], to_z(d))

        def zg_copy(q, d):
            own = full.at[q, at_own(mx, mz)]
            return remote(own, own, zg_send.at[base + q, d - 1], zg_recv.at[base + q, d - 1], to_z(d))

        def xg_copy(q, d):
            own = full.at[q, at_x(mx)]
            return remote(own, own, xg_send.at[base + q, d - 1], xg_recv.at[base + q, d - 1], to_x(d))

        def send_x(q):
            for d in range(1, X):
                begin(x_copy(q, d))

        def sum_x(q):
            for d in range(1, X):
                x_copy(q, d).wait_recv()
            total = part[q, at_x(mx)]
            for d in range(1, X):
                total += xrecv[q, d - 1]
            xred[q] = total
            for d in range(1, Z):
                begin(z_copy(q, d))

        def sum_z(q):
            for d in range(1, Z):
                z_copy(q, d).wait_recv()
            total = xred[q, at_z(mz)]
            for d in range(1, Z):
                total += zrecv[q, d - 1]
            full[q, at_own(mx, mz)] = total
            for d in range(1, Z):
                begin(zg_copy(q, d))

        def gather_x(q):
            for d in range(1, Z):
                zg_copy(q, d).wait_recv()
            for d in range(1, X):
                begin(xg_copy(q, d))

        def finish(q):
            for d in range(1, X):
                xg_copy(q, d).wait_recv()

        return send_x, sum_x, sum_z, gather_x, finish

    def pipeline(count, stages):
        for tick in range(count + LAGS[-1]):
            for lag, stage in zip(LAGS, stages):
                if 0 <= tick - lag < count:
                    stage(tick - lag)

    send_x, sum_x, sum_z, gather_x, finish = reducer(0, a_part, a_xrecv, a_xred, a_zrecv, a_full)

    def project(c):
        loads[c][0].wait()
        loads[c][1].wait()
        if c == 0:
            pin_load.wait()
            pout_load.wait()
        rows = pl.ds(c * TA, TA)
        a_part[c, :, :pj] = jnp.dot(xin[rows], pin[...], preferred_element_type=F32)
        a_part[c, :, pj:] = jnp.dot(gin[rows], pout[...], preferred_element_type=F32)
        send_x(c)

    def e_rows(t, c):
        return pl.ds(pl.multiple_of(t * ex_here + c * ex_chunk, ex_chunk), ex_chunk)

    def ey_copy(c, d):
        ref = e_all.at[e_rows(tensor, c)]
        other = lax.rem(my + d, Y) * CORES + mc
        return remote(ref, ref, ey_send.at[c, d - 1], ey_recv.at[c, d - 1], to_t(other))

    def ec_copy(c, d):
        source = lax.rem(my + Y - d, Y) * CORES + mc
        ref = e_all.at[e_rows(source, c)]
        return remote(ref, ref, ec_send.at[c, d], ec_recv.at[c, d], to_t(my * CORES + 1 - mc))

    tok_of = lax.broadcasted_iota(jnp.int32, (ex_chunk, TA), 1)
    first = lax.broadcasted_iota(jnp.int32, (ex_chunk, TA), 0) * TOK
    mask = jnp.logical_and(tok_of >= first, tok_of < first + TOK)

    def outer(c):
        finish(c)
        turned = jnp.transpose(a_full[c, :, pj:])
        for block in range(S):
            gt[c, block] = turned[block * ks:(block + 1) * ks]
        mine = gt[c, store]
        wide = jnp.where(mask[None], mine[:, None, :], 0.0).reshape(ks * ex_chunk, TA)
        sums = dot3(halves(wide), halves(a_full[c, :, :pj]), ((1,), (0,)))
        for k in range(ks):
            e_all[e_rows(tensor, c), k * pj:(k + 1) * pj] = sums[k * ex_chunk:(k + 1) * ex_chunk]
        for d in range(1, Y):
            begin(ey_copy(c, d))
        begin(ec_copy(c, 0))

    pipeline(NA, (project, sum_x, sum_z, gather_x, outer))
    for c in range(NA):
        for d in range(1, Y):
            ey_copy(c, d).wait_recv()
            begin(ec_copy(c, d))
    for c in range(NA):
        for d in range(Y):
            ec_copy(c, d).wait_recv()

    depth = e_all.shape[1]
    kt = min(512, depth)

    @pl.loop(0, depth // kt)
    def _(i):
        cols = pl.ds(pl.multiple_of(i * kt, kt), kt)
        high, low = halves(e_all[:, cols])
        e_hi[:, cols] = high
        e_lo[:, cols] = low

    bsend_x, bsum_x, bsum_z, bgather_x, bfinish = reducer(
        NA, b_part, b_xrecv, b_xred, b_zrecv, b_full
    )

    def precondition(q):
        slot = q % SLOTS
        f_load(q).wait()
        b_part[q] = jnp.zeros(b_part.shape[1:], F32)

        @pl.loop(0, depth // kt)
        def _(i):
            cols = pl.ds(pl.multiple_of(i * kt, kt), kt)
            b_part[q] += dot3(
                (e_hi[:, cols], e_lo[:, cols]), halves(fbuf[slot, cols, :]), ((1,), (0,))
            )

        bsend_x(q)
        if q + SLOTS < NB:
            f_load(q + SLOTS).start()

    def add_scores(q):
        bfinish(q)
        if q == 0:
            s_load.wait()
        term = dot3(
            halves(b_full[q]), halves(sbuf[:, pl.ds(q * CW, CW)]), ((1,), (1,))
        )
        if q == 0:
            score[...] = term
        else:
            score[...] += term

    pipeline(NB, (precondition, bsum_x, bsum_z, bgather_x, add_scores))

    def s_rows(t):
        return pl.ds(pl.multiple_of(t * ex_here, ex_here), ex_here)

    def sc_copy(d):
        other = lax.rem(tensor + d, T)
        return remote(score.at[s_rows(other)], srecv.at[d - 1],
                      sc_send.at[d - 1], sc_recv.at[d - 1], to_t(other))

    for d in range(1, T):
        begin(sc_copy(d))
    total = score[s_rows(tensor)]
    for d in range(1, T):
        sc_copy(d).wait_recv()
        total += srecv[d - 1]
    out_ref[...] = total
    for copy in pending:
        copy.wait_send()


def on_device(mesh_shape, inputs, out_grads, proj_in, proj_out, inv_fisher, store_grads):
    T, S = mesh_shape["tensor"], mesh_shape["store"]
    Y = T // CORES
    X = Y if S % Y == 0 else 1
    Z = S // X
    examples, tok, width = inputs.shape
    rows = examples * tok
    flat_inputs = inputs.reshape(rows, width)
    flat_grads = out_grads.reshape(rows, out_grads.shape[2])
    TA = min(rows, max(256, 8 * S))
    NA = rows // TA
    depth, columns = inv_fisher.shape
    CW = min(512, columns)
    NB = columns // CW
    pj, pk = proj_in.shape[1], proj_out.shape[1]
    stored = store_grads.shape[0]
    ex_all = examples * T
    both = pj + pk
    cfg = dict(X=X, Z=Z, T=T, Y=Y, NA=NA, NB=NB, TA=TA, CW=CW, TOK=tok)
    NQ = NA + NB
    dma = pltpu.SemaphoreType.DMA
    vmem = pltpu.VMEM
    scratch = [
        vmem(flat_inputs.shape, BF16), vmem(flat_grads.shape, BF16),
        vmem(proj_in.shape, BF16), vmem(proj_out.shape, BF16),
        vmem((min(SLOTS, NB), depth, CW), F32), vmem(store_grads.shape, F32),
        vmem((NA, TA, both), F32), vmem((NA, X - 1, TA // X, both), F32),
        vmem((NA, TA // X, both), F32), vmem((NA, Z - 1, TA // S, both), F32),
        vmem((NA, TA, both), F32), vmem((NA, S, pk // S, TA), F32),
        vmem((ex_all, depth), F32), vmem((ex_all, depth), BF16), vmem((ex_all, depth), BF16),
        vmem((NB, ex_all, CW), F32), vmem((NB, X - 1, ex_all // X, CW), F32),
        vmem((NB, ex_all // X, CW), F32), vmem((NB, Z - 1, ex_all // S, CW), F32),
        vmem((NB, ex_all, CW), F32),
        vmem((ex_all, stored), F32), vmem((T - 1, examples, stored), F32),
        dma((NA, 2)), dma((2,)), dma((min(SLOTS, NB),)), dma((1,)),
        dma((NQ, X - 1)), dma((NQ, X - 1)), dma((NQ, Z - 1)), dma((NQ, Z - 1)),
        dma((NQ, Z - 1)), dma((NQ, Z - 1)), dma((NQ, X - 1)), dma((NQ, X - 1)),
        dma((NA, max(Y - 1, 1))), dma((NA, max(Y - 1, 1))), dma((NA, Y)), dma((NA, Y)),
        dma((T - 1,)), dma((T - 1,)),
    ]
    hbm = pl.BlockSpec(memory_space=pl.ANY)
    return pl.pallas_call(
        functools.partial(kernel, cfg),
        out_shape=jax.ShapeDtypeStruct((examples, stored), F32),
        in_specs=[hbm] * 6,
        out_specs=pl.BlockSpec(memory_space=pltpu.VMEM),
        scratch_shapes=scratch,
        compiler_params=pltpu.CompilerParams(
            collective_id=0, has_side_effects=True, vmem_limit_bytes=60 * 1024 * 1024
        ),
    )(flat_inputs, flat_grads, proj_in, proj_out, inv_fisher, store_grads)


def solution(mesh):
    placed = (
        P("tensor", None, "store"),
        P("tensor", None, "store"),
        P("store", None),
        P("store", None),
        P("store", "tensor"),
        P("store", "tensor"),
    )
    return jax.shard_map(
        functools.partial(on_device, dict(mesh.shape)), mesh=mesh, in_specs=placed,
        out_specs=P("tensor", "store"), check_vma=False,
    )
```

```python
import functools
import jax
import jax.numpy as jnp
from jax import lax
from jax.experimental import pallas as pl
from jax.experimental.pallas import tpu as pltpu
from jax.sharding import PartitionSpec as P

F32 = jnp.float32
BF16 = jnp.bfloat16
MESH = pl.DeviceIdType.MESH
CORES = 2
A_LAGS = (0, 1, 2, 3, 4, 5)
B_LAGS = (0, 2, 3, 4, 5)
SLOTS = 4


def halves(value):
    high = value.astype(BF16)
    low = (value - high.astype(F32)).astype(BF16)
    return high, low


def dot3(left, right, dims):
    lh, ll = left
    rh, rl = right
    dot = functools.partial(
        lax.dot_general, dimension_numbers=(dims, ((), ())), preferred_element_type=F32
    )
    return dot(lh, rh) + (dot(lh, rl) + dot(ll, rh))


def kernel(
    cfg,
    x_hbm, g_hbm, pin_hbm, pout_hbm, f_hbm, s_hbm, out_ref,
    xin, gin, pin, pout, fbuf, sbuf,
    a_part, a_xrecv, a_red, a_zrecv, a_full, gt,
    e_all, e_hi, e_lo,
    b_part, b_xrecv, b_red, b_zrecv, b_full,
    score, trecv, xpart, xrecv,
    in_sem, proj_sem, f_sem, s_sem,
    xs_send, xs_recv, zs_send, zs_recv, zg_send, zg_recv, xg_send, xg_recv,
    ey_send, ey_recv, ec_send, ec_recv, st_send, st_recv, sc_send, sc_recv, sx_send, sx_recv,
):
    X, Z, T, Y = cfg["X"], cfg["Z"], cfg["T"], cfg["Y"]
    NA, NB, TA, CW, TOK = cfg["NA"], cfg["NB"], cfg["TA"], cfg["CW"], cfg["TOK"]
    S = X * Z
    store, tensor = lax.axis_index("store"), lax.axis_index("tensor")
    mx, mz = lax.rem(store, X), store // X
    my, mc = tensor // CORES, lax.rem(tensor, CORES)
    pj = pin.shape[1]
    pk = pout.shape[1]
    ks = pk // S
    ex_here = xin.shape[0] // TOK
    ex_all = e_all.shape[0]
    ex_chunk = TA // TOK

    def xpeer(d):
        return lax.rem(mx + d, X)

    def zpeer(d):
        return lax.rem(mz + d, Z)

    def to_x(d):
        return {"store": mz * X + xpeer(d), "tensor": tensor}

    def to_z(d):
        return {"store": zpeer(d) * X + mx, "tensor": tensor}

    def to_t(t):
        return {"store": store, "tensor": t}

    def remote(src, dst, send, recv, device):
        return pltpu.make_async_remote_copy(
            src_ref=src, dst_ref=dst, send_sem=send, recv_sem=recv,
            device_id=device, device_id_type=MESH,
        )

    loads = []
    for c in range(NA):
        rows = pl.ds(c * TA, TA)
        loads.append((
            pltpu.make_async_copy(x_hbm.at[rows], xin.at[rows], in_sem.at[c, 0]),
            pltpu.make_async_copy(g_hbm.at[rows], gin.at[rows], in_sem.at[c, 1]),
        ))
    pin_load = pltpu.make_async_copy(pin_hbm, pin, proj_sem.at[0])
    pout_load = pltpu.make_async_copy(pout_hbm, pout, proj_sem.at[1])
    CX = s_hbm.shape[1] // X
    WX = CW // X

    def s_columns(x, q):
        return pl.ds(pl.multiple_of(x * CX + q * WX, WX), WX)

    def s_load(q):
        return pltpu.make_async_copy(
            s_hbm.at[:, s_columns(mx, q)], sbuf.at[q, mx], s_sem.at[q]
        )

    def s_copy(q, d):
        return remote(s_hbm.at[:, s_columns(xpeer(d), q)], sbuf.at[q, mx],
                      st_send.at[q, d - 1], st_recv.at[q, d - 1], to_x(d))

    def s_arrival(q, d):
        source = lax.rem(mx + X - d, X)
        return remote(sbuf.at[q, source], sbuf.at[q, source],
                      st_send.at[q, d - 1], st_recv.at[q, d - 1], to_x(d))

    pin_load.start()
    pout_load.start()
    for pair in loads:
        pair[0].start()
        pair[1].start()

    def f_load(q, x):
        slot = q % SLOTS
        return pltpu.make_async_copy(
            f_hbm.at[:, pl.ds(x * CX + q * WX, WX)], fbuf.at[slot, x], f_sem.at[slot, x]
        )

    for q in range(min(SLOTS, NB)):
        for x in range(X):
            f_load(q, x).start()
    for q in range(NB):
        s_load(q).start()

    barrier = pltpu.get_barrier_semaphore()
    for d in range(1, X):
        pl.semaphore_signal(barrier, inc=1, device_id=to_x(d), device_id_type=MESH)
    for d in range(1, Z):
        pl.semaphore_signal(barrier, inc=1, device_id=to_z(d), device_id_type=MESH)
    for d in range(1, T):
        pl.semaphore_signal(
            barrier, inc=1, device_id=to_t(lax.rem(tensor + d, T)), device_id_type=MESH
        )
    pl.semaphore_wait(barrier, X + Z + T - 3)

    pending = []

    def begin(copy):
        copy.start()
        pending.append(copy)

    half = Z // 2
    lower = mz < half
    inward = jnp.where(lower, mz + 1, mz - 1)
    outward = jnp.where(lower, mz - 1, mz + 1)
    from_middle = jnp.where(lower, half - 1 - mz, mz - half)
    is_middle = from_middle == 0
    is_end = from_middle == half - 1
    slot_there = jnp.where(is_middle, 1, 0)
    to_in = {"store": inward * X + mx, "tensor": tensor}
    to_out = {"store": outward * X + mx, "tensor": tensor}
    finals = []

    def tree(base, red, zrecv, result):
        def inward_copy(q):
            return remote(red.at[q], zrecv.at[q, slot_there],
                          zs_send.at[base + q], zs_recv.at[base + q, slot_there], to_in)

        def arrival(q, slot):
            return remote(red.at[q], zrecv.at[q, slot],
                          zs_send.at[base + q], zs_recv.at[base + q, slot], to_in)

        def outward_copy(q):
            return remote(result(q), result(q), zg_send.at[base + q], zg_recv.at[base + q], to_out)

        def enter(q):
            @pl.when(is_end)
            def _():
                inward_copy(q).start()

        def up(q):
            @pl.when(jnp.logical_not(is_end))
            def _():
                arrival(q, 0).wait_recv()
                red[q] += zrecv[q, 0]
                inward_copy(q).start()

        def middle(q):
            @pl.when(is_middle)
            def _():
                arrival(q, 1).wait_recv()
                result(q)[...] = red[q] + zrecv[q, 1]
                if half > 1:
                    outward_copy(q).start()

        def down(q):
            @pl.when(jnp.logical_not(is_middle))
            def _():
                outward_copy(q).wait_recv()

                @pl.when(jnp.logical_not(is_end))
                def _():
                    outward_copy(q).start()

        def drain(count):
            for q in range(count):
                inward_copy(q).wait_send()

            @pl.when(jnp.logical_not(is_end))
            def _():
                for q in range(count):
                    outward_copy(q).wait_send()

        finals.append(drain)
        return enter, up, middle, down

    def pipeline(count, lags, stages, beside=None):
        for tick in range(count + lags[-1]):
            for lag, stage in zip(lags, stages):
                if 0 <= tick - lag < count:
                    stage(tick - lag)
            if beside is not None:
                beside(tick)

    rx = TA // X

    def at_x(p):
        return pl.ds(pl.multiple_of(p * rx, rx), rx)

    def a_total(c):
        return a_full.at[c, at_x(mx)]

    a_enter, a_up, a_middle, a_down = tree(0, a_red, a_zrecv, a_total)

    def ax_copy(c, d):
        return remote(a_part.at[c, at_x(xpeer(d))], a_xrecv.at[c, d - 1],
                      xs_send.at[c, d - 1], xs_recv.at[c, d - 1], to_x(d))

    def xg_copy(c, d):
        return remote(a_total(c), a_total(c),
                      xg_send.at[c, d - 1], xg_recv.at[c, d - 1], to_x(d))

    def a_sum_x(c):
        for d in range(1, X):
            ax_copy(c, d).wait_recv()
        total = a_part[c, at_x(mx)]
        for d in range(1, X):
            total += a_xrecv[c, d - 1]
        a_red[c] = total
        a_enter(c)

    def a_gather_x(c):
        a_down(c)
        for d in range(1, X):
            begin(xg_copy(c, d))

    def project(c):
        loads[c][0].wait()
        loads[c][1].wait()
        if c == 0:
            pin_load.wait()
            pout_load.wait()
        rows = pl.ds(c * TA, TA)
        a_part[c, :, :pj] = jnp.dot(xin[rows], pin[...], preferred_element_type=F32)
        a_part[c, :, pj:] = jnp.dot(gin[rows], pout[...], preferred_element_type=F32)
        for d in range(1, X):
            begin(ax_copy(c, d))

    def e_rows(t, c):
        return pl.ds(pl.multiple_of(t * ex_here + c * ex_chunk, ex_chunk), ex_chunk)

    def ey_copy(c, d):
        ref = e_all.at[e_rows(tensor, c)]
        other = lax.rem(my + d, Y) * CORES + mc
        return remote(ref, ref, ey_send.at[c, d - 1], ey_recv.at[c, d - 1], to_t(other))

    def ec_copy(c, d):
        source = lax.rem(my + Y - d, Y) * CORES + mc
        ref = e_all.at[e_rows(source, c)]
        return remote(ref, ref, ec_send.at[c, d], ec_recv.at[c, d], to_t(my * CORES + 1 - mc))

    tok_of = lax.broadcasted_iota(jnp.int32, (ex_chunk, TA), 1)
    first = lax.broadcasted_iota(jnp.int32, (ex_chunk, TA), 0) * TOK
    mask = jnp.logical_and(tok_of >= first, tok_of < first + TOK)

    def outer(c):
        for d in range(1, X):
            xg_copy(c, d).wait_recv()
        turned = jnp.transpose(a_full[c, :, pj:])
        for block in range(S):
            gt[c, block] = turned[block * ks:(block + 1) * ks]
        mine = gt[c, store]
        wide = jnp.where(mask[None], mine[:, None, :], 0.0).reshape(ks * ex_chunk, TA)
        sums = dot3(halves(wide), halves(a_full[c, :, :pj]), ((1,), (0,)))
        for k in range(ks):
            e_all[e_rows(tensor, c), k * pj:(k + 1) * pj] = sums[k * ex_chunk:(k + 1) * ex_chunk]
        for d in range(1, Y):
            begin(ey_copy(c, d))
        begin(ec_copy(c, 0))

    def store_columns(tick):
        if tick >= A_LAGS[1] and tick - A_LAGS[1] < NB:
            for d in range(1, X):
                begin(s_copy(tick - A_LAGS[1], d))

    pipeline(NA, A_LAGS, (project, a_sum_x, a_up, a_middle, a_gather_x, outer), store_columns)
    for q in range(NA + A_LAGS[-1] - A_LAGS[1], NB):
        for d in range(1, X):
            begin(s_copy(q, d))
    for c in range(NA):
        for d in range(1, Y):
            ey_copy(c, d).wait_recv()
            begin(ec_copy(c, d))
    for c in range(NA):
        for d in range(Y):
            ec_copy(c, d).wait_recv()

    depth = e_all.shape[1]
    kt = min(512, depth)

    @pl.loop(0, depth // kt)
    def _(i):
        cols = pl.ds(pl.multiple_of(i * kt, kt), kt)
        high, low = halves(e_all[:, cols])
        e_hi[:, cols] = high
        e_lo[:, cols] = low

    b_enter, b_up, b_middle, b_down = tree(NA, b_red, b_zrecv, lambda q: b_full.at[q])

    def bx_copy(q, d):
        return remote(b_part.at[q, xpeer(d)], b_xrecv.at[q, d - 1],
                      xs_send.at[NA + q, d - 1], xs_recv.at[NA + q, d - 1], to_x(d))

    def precondition(q):
        slot = q % SLOTS
        for x in range(X):
            f_load(q, x).wait()
        for x in range(X):
            b_part[q, x] = jnp.zeros(b_part.shape[2:], F32)

            @pl.loop(0, depth // kt)
            def _(i):
                cols = pl.ds(pl.multiple_of(i * kt, kt), kt)
                b_part[q, x] += dot3(
                    (e_hi[:, cols], e_lo[:, cols]), halves(fbuf[slot, x, cols, :]), ((1,), (0,))
                )

        for d in range(1, X):
            begin(bx_copy(q, d))
        if q + SLOTS < NB:
            for x in range(X):
                f_load(q + SLOTS, x).start()

    def b_sum_x(q):
        for d in range(1, X):
            bx_copy(q, d).wait_recv()
        total = b_part[q, mx]
        for d in range(1, X):
            total += b_xrecv[q, d - 1]
        b_red[q] = total
        b_enter(q)

    def add_scores(q):
        b_down(q)
        s_load(q).wait()
        for d in range(1, X):
            s_arrival(q, d).wait_recv()
        left = halves(b_full[q])
        for x in range(X):
            term = dot3(left, halves(sbuf[q, x]), ((1,), (1,)))
            if q == 0:
                score[x] = term
            else:
                score[x] += term

    pipeline(NB, B_LAGS, (precondition, b_sum_x, b_up, b_middle, add_scores))

    def s_rows(t):
        return pl.ds(pl.multiple_of(t * ex_here, ex_here), ex_here)

    def sc_copy(d):
        other = lax.rem(tensor + d, T)
        return remote(score.at[:, s_rows(other)], trecv.at[d - 1],
                      sc_send.at[d - 1], sc_recv.at[d - 1], to_t(other))

    def sx_copy(d):
        return remote(xpart.at[xpeer(d)], xrecv.at[d - 1],
                      sx_send.at[d - 1], sx_recv.at[d - 1], to_x(d))

    for d in range(1, T):
        begin(sc_copy(d))
    total = score[:, s_rows(tensor)]
    for d in range(1, T):
        sc_copy(d).wait_recv()
        total += trecv[d - 1]
    xpart[...] = total
    for d in range(1, X):
        begin(sx_copy(d))
    total = xpart[mx]
    for d in range(1, X):
        sx_copy(d).wait_recv()
        total += xrecv[d - 1]
    out_ref[...] = total
    finals[0](NA)
    finals[1](NB)
    for copy in pending:
        copy.wait_send()


def on_device(mesh_shape, inputs, out_grads, proj_in, proj_out, inv_fisher, store_grads):
    T, S = mesh_shape["tensor"], mesh_shape["store"]
    Y = T // CORES
    X = Y if S % Y == 0 else 1
    Z = S // X
    examples, tok, width = inputs.shape
    rows = examples * tok
    flat_inputs = inputs.reshape(rows, width)
    flat_grads = out_grads.reshape(rows, out_grads.shape[2])
    TA = min(rows, max(256, 8 * S))
    NA = rows // TA
    depth, columns = inv_fisher.shape
    CW = min(512, columns)
    NB = columns // CW
    pj, pk = proj_in.shape[1], proj_out.shape[1]
    stored = store_grads.shape[0]
    ex_all = examples * T
    both = pj + pk
    cfg = dict(X=X, Z=Z, T=T, Y=Y, NA=NA, NB=NB, TA=TA, CW=CW, TOK=tok)
    NQ = NA + NB
    dma = pltpu.SemaphoreType.DMA
    vmem = pltpu.VMEM
    scratch = [
        vmem(flat_inputs.shape, BF16), vmem(flat_grads.shape, BF16),
        vmem(proj_in.shape, BF16), vmem(proj_out.shape, BF16),
        vmem((min(SLOTS, NB), X, depth, CW // X), F32),
        vmem((NB, X, stored, CW // X), F32),
        vmem((NA, TA, both), F32), vmem((NA, X - 1, TA // X, both), F32),
        vmem((NA, TA // X, both), F32), vmem((NA, 2, TA // X, both), F32),
        vmem((NA, TA, both), F32), vmem((NA, S, pk // S, TA), F32),
        vmem((ex_all, depth), F32), vmem((ex_all, depth), BF16), vmem((ex_all, depth), BF16),
        vmem((NB, X, ex_all, CW // X), F32), vmem((NB, X - 1, ex_all, CW // X), F32),
        vmem((NB, ex_all, CW // X), F32), vmem((NB, 2, ex_all, CW // X), F32),
        vmem((NB, ex_all, CW // X), F32),
        vmem((X, ex_all, stored), F32), vmem((T - 1, X, examples, stored), F32),
        vmem((X, examples, stored), F32), vmem((X - 1, examples, stored), F32),
        dma((NA, 2)), dma((2,)), dma((min(SLOTS, NB), X)), dma((NB,)),
        dma((NQ, X - 1)), dma((NQ, X - 1)), dma((NQ,)), dma((NQ, 2)),
        dma((NQ,)), dma((NQ,)), dma((NA, X - 1)), dma((NA, X - 1)),
        dma((NA, max(Y - 1, 1))), dma((NA, max(Y - 1, 1))), dma((NA, Y)), dma((NA, Y)),
        dma((NB, X - 1)), dma((NB, X - 1)), dma((T - 1,)), dma((T - 1,)),
        dma((X - 1,)), dma((X - 1,)),
    ]
    hbm = pl.BlockSpec(memory_space=pl.ANY)
    return pl.pallas_call(
        functools.partial(kernel, cfg),
        out_shape=jax.ShapeDtypeStruct((examples, stored), F32),
        in_specs=[hbm] * 6,
        out_specs=pl.BlockSpec(memory_space=pltpu.VMEM),
        scratch_shapes=scratch,
        compiler_params=pltpu.CompilerParams(
            collective_id=0, has_side_effects=True, vmem_limit_bytes=60 * 1024 * 1024
        ),
    )(flat_inputs, flat_grads, proj_in, proj_out, inv_fisher, store_grads)


def solution(mesh):
    placed = (
        P("tensor", None, "store"),
        P("tensor", None, "store"),
        P("store", None),
        P("store", None),
        P("store", "tensor"),
        P("store", "tensor"),
    )
    return jax.shard_map(
        functools.partial(on_device, dict(mesh.shape)), mesh=mesh, in_specs=placed,
        out_specs=P("tensor", "store"), check_vma=False,
    )
```

```python
import functools
import jax
import jax.numpy as jnp
from jax import lax
from jax.experimental import pallas as pl
from jax.experimental.pallas import tpu as pltpu
from jax.sharding import PartitionSpec as P

F32 = jnp.float32
BF16 = jnp.bfloat16
MESH = pl.DeviceIdType.MESH
CORES = 2
A_LAGS = (0, 1, 2, 3, 4, 5)
B_LAGS = (0, 2, 3, 4, 5)
SLOTS = 4
EARLY = 2


def halves(value):
    high = value.astype(BF16)
    low = (value - high.astype(F32)).astype(BF16)
    return high, low


def dot3(left, right, dims):
    lh, ll = left
    rh, rl = right
    dot = functools.partial(
        lax.dot_general, dimension_numbers=(dims, ((), ())), preferred_element_type=F32
    )
    return dot(lh, rh) + (dot(lh, rl) + dot(ll, rh))


def kernel(
    cfg,
    x_hbm, g_hbm, pin_hbm, pout_hbm, f_hbm, s_hbm, out_ref,
    xin, gin, pin, pout, fbuf, sbuf,
    a_part, a_xrecv, a_red, a_zrecv, a_full, gt,
    e_all, e_hi, e_lo,
    b_part, b_xrecv, b_red, b_zrecv, b_full,
    score, trecv, xpart, xrecv,
    in_sem, proj_sem, f_sem, s_sem,
    xs_send, xs_recv, zs_send, zs_recv, zg_send, zg_recv, xg_send, xg_recv,
    ey_send, ey_recv, ec_send, ec_recv, st_send, st_recv, sc_send, sc_recv, sx_send, sx_recv,
):
    X, Z, T, Y = cfg["X"], cfg["Z"], cfg["T"], cfg["Y"]
    NA, NB, TA, CW, TOK = cfg["NA"], cfg["NB"], cfg["TA"], cfg["CW"], cfg["TOK"]
    S = X * Z
    store, tensor = lax.axis_index("store"), lax.axis_index("tensor")
    mx, mz = lax.rem(store, X), store // X
    my, mc = tensor // CORES, lax.rem(tensor, CORES)
    pj = pin.shape[1]
    pk = pout.shape[1]
    ks = pk // S
    ex_here = xin.shape[0] // TOK
    ex_all = e_all.shape[0]
    ex_chunk = TA // TOK

    def xpeer(d):
        return lax.rem(mx + d, X)

    def zpeer(d):
        return lax.rem(mz + d, Z)

    def to_x(d):
        return {"store": mz * X + xpeer(d), "tensor": tensor}

    def to_z(d):
        return {"store": zpeer(d) * X + mx, "tensor": tensor}

    def to_t(t):
        return {"store": store, "tensor": t}

    def remote(src, dst, send, recv, device):
        return pltpu.make_async_remote_copy(
            src_ref=src, dst_ref=dst, send_sem=send, recv_sem=recv,
            device_id=device, device_id_type=MESH,
        )

    loads = []
    for c in range(NA):
        rows = pl.ds(c * TA, TA)
        loads.append((
            pltpu.make_async_copy(x_hbm.at[rows], xin.at[rows], in_sem.at[c, 0]),
            pltpu.make_async_copy(g_hbm.at[rows], gin.at[rows], in_sem.at[c, 1]),
        ))
    pin_load = pltpu.make_async_copy(pin_hbm, pin, proj_sem.at[0])
    pout_load = pltpu.make_async_copy(pout_hbm, pout, proj_sem.at[1])
    CX = s_hbm.shape[1] // X
    WX = CW // X

    def s_columns(x, q):
        return pl.ds(pl.multiple_of(x * CX + q * WX, WX), WX)

    def s_load(q):
        return pltpu.make_async_copy(
            s_hbm.at[:, s_columns(mx, q)], sbuf.at[q, mx], s_sem.at[q]
        )

    def s_copy(q, d):
        return remote(s_hbm.at[:, s_columns(xpeer(d), q)], sbuf.at[q, mx],
                      st_send.at[q, d - 1], st_recv.at[q, d - 1], to_x(d))

    def s_arrival(q, d):
        source = lax.rem(mx + X - d, X)
        return remote(sbuf.at[q, source], sbuf.at[q, source],
                      st_send.at[q, d - 1], st_recv.at[q, d - 1], to_x(d))

    pin_load.start()
    pout_load.start()
    for pair in loads:
        pair[0].start()
        pair[1].start()

    def f_load(q, x):
        slot = q % SLOTS
        return pltpu.make_async_copy(
            f_hbm.at[:, pl.ds(x * CX + q * WX, WX)], fbuf.at[slot, x], f_sem.at[slot, x]
        )

    for q in range(min(SLOTS, NB)):
        for x in range(X):
            f_load(q, x).start()
    for q in range(NB):
        s_load(q).start()

    barrier = pltpu.get_barrier_semaphore()
    for d in range(1, X):
        pl.semaphore_signal(barrier, inc=1, device_id=to_x(d), device_id_type=MESH)
    for d in range(1, Z):
        pl.semaphore_signal(barrier, inc=1, device_id=to_z(d), device_id_type=MESH)
    for d in range(1, T):
        pl.semaphore_signal(
            barrier, inc=1, device_id=to_t(lax.rem(tensor + d, T)), device_id_type=MESH
        )
    pl.semaphore_wait(barrier, X + Z + T - 3)

    pending = []

    def begin(copy):
        copy.start()
        pending.append(copy)

    half = Z // 2
    lower = mz < half
    inward = jnp.where(lower, mz + 1, mz - 1)
    outward = jnp.where(lower, mz - 1, mz + 1)
    from_middle = jnp.where(lower, half - 1 - mz, mz - half)
    is_middle = from_middle == 0
    is_end = from_middle == half - 1
    slot_there = jnp.where(is_middle, 1, 0)
    to_in = {"store": inward * X + mx, "tensor": tensor}
    to_out = {"store": outward * X + mx, "tensor": tensor}
    finals = []

    def tree(base, red, zrecv, result):
        def inward_copy(q):
            return remote(red.at[q], zrecv.at[q, slot_there],
                          zs_send.at[base + q], zs_recv.at[base + q, slot_there], to_in)

        def arrival(q, slot):
            return remote(red.at[q], zrecv.at[q, slot],
                          zs_send.at[base + q], zs_recv.at[base + q, slot], to_in)

        def outward_copy(q):
            return remote(result(q), result(q), zg_send.at[base + q], zg_recv.at[base + q], to_out)

        def enter(q):
            @pl.when(is_end)
            def _():
                inward_copy(q).start()

        def up(q):
            @pl.when(jnp.logical_not(is_end))
            def _():
                arrival(q, 0).wait_recv()
                red[q] += zrecv[q, 0]
                inward_copy(q).start()

        def middle(q):
            @pl.when(is_middle)
            def _():
                arrival(q, 1).wait_recv()
                result(q)[...] = red[q] + zrecv[q, 1]
                if half > 1:
                    outward_copy(q).start()

        def down(q):
            @pl.when(jnp.logical_not(is_middle))
            def _():
                outward_copy(q).wait_recv()

                @pl.when(jnp.logical_not(is_end))
                def _():
                    outward_copy(q).start()

        def drain(count):
            for q in range(count):
                inward_copy(q).wait_send()

            @pl.when(jnp.logical_not(is_end))
            def _():
                for q in range(count):
                    outward_copy(q).wait_send()

        finals.append(drain)
        return enter, up, middle, down

    def pipeline(count, lags, stages, beside=None):
        for tick in range(count + lags[-1]):
            for lag, stage in zip(lags, stages):
                if 0 <= tick - lag < count:
                    stage(tick - lag)
            if beside is not None:
                beside(tick)

    rx = TA // X

    def at_x(p):
        return pl.ds(pl.multiple_of(p * rx, rx), rx)

    def a_total(c):
        return a_full.at[c, at_x(mx)]

    a_enter, a_up, a_middle, a_down = tree(0, a_red, a_zrecv, a_total)

    def ax_copy(c, d):
        return remote(a_part.at[c, at_x(xpeer(d))], a_xrecv.at[c, d - 1],
                      xs_send.at[c, d - 1], xs_recv.at[c, d - 1], to_x(d))

    def xg_copy(c, d):
        return remote(a_total(c), a_total(c),
                      xg_send.at[c, d - 1], xg_recv.at[c, d - 1], to_x(d))

    def a_sum_x(c):
        for d in range(1, X):
            ax_copy(c, d).wait_recv()
        total = a_part[c, at_x(mx)]
        for d in range(1, X):
            total += a_xrecv[c, d - 1]
        a_red[c] = total
        a_enter(c)

    def a_gather_x(c):
        a_down(c)
        for d in range(1, X):
            begin(xg_copy(c, d))

    def project(c):
        loads[c][0].wait()
        loads[c][1].wait()
        if c == 0:
            pin_load.wait()
            pout_load.wait()
        rows = pl.ds(c * TA, TA)
        a_part[c, :, :pj] = jnp.dot(xin[rows], pin[...], preferred_element_type=F32)
        a_part[c, :, pj:] = jnp.dot(gin[rows], pout[...], preferred_element_type=F32)
        for d in range(1, X):
            begin(ax_copy(c, d))

    def e_rows(t, c):
        return pl.ds(pl.multiple_of(t * ex_here + c * ex_chunk, ex_chunk), ex_chunk)

    def ey_copy(c, d):
        ref = e_all.at[e_rows(tensor, c)]
        other = lax.rem(my + d, Y) * CORES + mc
        return remote(ref, ref, ey_send.at[c, d - 1], ey_recv.at[c, d - 1], to_t(other))

    def ec_copy(c, d):
        source = lax.rem(my + Y - d, Y) * CORES + mc
        ref = e_all.at[e_rows(source, c)]
        return remote(ref, ref, ec_send.at[c, d], ec_recv.at[c, d], to_t(my * CORES + 1 - mc))

    tok_of = lax.broadcasted_iota(jnp.int32, (ex_chunk, TA), 1)
    first = lax.broadcasted_iota(jnp.int32, (ex_chunk, TA), 0) * TOK
    mask = jnp.logical_and(tok_of >= first, tok_of < first + TOK)

    def outer(c):
        for d in range(1, X):
            xg_copy(c, d).wait_recv()
        turned = jnp.transpose(a_full[c, :, pj:])
        for block in range(S):
            gt[c, block] = turned[block * ks:(block + 1) * ks]
        mine = gt[c, store]
        wide = jnp.where(mask[None], mine[:, None, :], 0.0).reshape(ks * ex_chunk, TA)
        sums = dot3(halves(wide), halves(a_full[c, :, :pj]), ((1,), (0,)))
        for k in range(ks):
            e_all[e_rows(tensor, c), k * pj:(k + 1) * pj] = sums[k * ex_chunk:(k + 1) * ex_chunk]
        for d in range(1, Y):
            begin(ey_copy(c, d))
        begin(ec_copy(c, 0))

    def store_columns(tick):
        if EARLY <= tick + EARLY < NB:
            for d in range(1, X):
                begin(s_copy(tick + EARLY, d))

    for q in range(min(EARLY, NB)):
        for d in range(1, X):
            begin(s_copy(q, d))

    pipeline(NA, A_LAGS, (project, a_sum_x, a_up, a_middle, a_gather_x, outer), store_columns)
    for q in range(NA + A_LAGS[-1] + EARLY, NB):
        for d in range(1, X):
            begin(s_copy(q, d))
    for c in range(NA):
        for d in range(1, Y):
            ey_copy(c, d).wait_recv()
            begin(ec_copy(c, d))
    for c in range(NA):
        for d in range(Y):
            ec_copy(c, d).wait_recv()

    depth = e_all.shape[1]
    kt = min(512, depth)

    @pl.loop(0, depth // kt)
    def _(i):
        cols = pl.ds(pl.multiple_of(i * kt, kt), kt)
        high, low = halves(e_all[:, cols])
        e_hi[:, cols] = high
        e_lo[:, cols] = low

    b_enter, b_up, b_middle, b_down = tree(NA, b_red, b_zrecv, lambda q: b_full.at[q])

    def bx_copy(q, d):
        return remote(b_part.at[q, xpeer(d)], b_xrecv.at[q, d - 1],
                      xs_send.at[NA + q, d - 1], xs_recv.at[NA + q, d - 1], to_x(d))

    def precondition(q):
        slot = q % SLOTS
        for x in range(X):
            f_load(q, x).wait()
        for x in range(X):
            b_part[q, x] = jnp.zeros(b_part.shape[2:], F32)

            @pl.loop(0, depth // kt)
            def _(i):
                cols = pl.ds(pl.multiple_of(i * kt, kt), kt)
                b_part[q, x] += dot3(
                    (e_hi[:, cols], e_lo[:, cols]), halves(fbuf[slot, x, cols, :]), ((1,), (0,))
                )

        for d in range(1, X):
            begin(bx_copy(q, d))
        if q + SLOTS < NB:
            for x in range(X):
                f_load(q + SLOTS, x).start()

    def b_sum_x(q):
        for d in range(1, X):
            bx_copy(q, d).wait_recv()
        total = b_part[q, mx]
        for d in range(1, X):
            total += b_xrecv[q, d - 1]
        b_red[q] = total
        b_enter(q)

    def add_scores(q):
        b_down(q)
        s_load(q).wait()
        for d in range(1, X):
            s_arrival(q, d).wait_recv()
        left = halves(b_full[q])
        for x in range(X):
            term = dot3(left, halves(sbuf[q, x]), ((1,), (1,)))
            if q == 0:
                score[x] = term
            else:
                score[x] += term

    pipeline(NB, B_LAGS, (precondition, b_sum_x, b_up, b_middle, add_scores))

    def s_rows(t):
        return pl.ds(pl.multiple_of(t * ex_here, ex_here), ex_here)

    def sc_copy(d):
        other = lax.rem(tensor + d, T)
        return remote(score.at[:, s_rows(other)], trecv.at[d - 1],
                      sc_send.at[d - 1], sc_recv.at[d - 1], to_t(other))

    def sx_copy(d):
        return remote(xpart.at[xpeer(d)], xrecv.at[d - 1],
                      sx_send.at[d - 1], sx_recv.at[d - 1], to_x(d))

    for d in range(1, T):
        begin(sc_copy(d))
    total = score[:, s_rows(tensor)]
    for d in range(1, T):
        sc_copy(d).wait_recv()
        total += trecv[d - 1]
    xpart[...] = total
    for d in range(1, X):
        begin(sx_copy(d))
    total = xpart[mx]
    for d in range(1, X):
        sx_copy(d).wait_recv()
        total += xrecv[d - 1]
    out_ref[...] = total
    finals[0](NA)
    finals[1](NB)
    for copy in pending:
        copy.wait_send()


def on_device(mesh_shape, inputs, out_grads, proj_in, proj_out, inv_fisher, store_grads):
    T, S = mesh_shape["tensor"], mesh_shape["store"]
    Y = T // CORES
    X = Y if S % Y == 0 else 1
    Z = S // X
    examples, tok, width = inputs.shape
    rows = examples * tok
    flat_inputs = inputs.reshape(rows, width)
    flat_grads = out_grads.reshape(rows, out_grads.shape[2])
    TA = min(rows, max(256, 8 * S))
    NA = rows // TA
    depth, columns = inv_fisher.shape
    CW = min(512, columns)
    NB = columns // CW
    pj, pk = proj_in.shape[1], proj_out.shape[1]
    stored = store_grads.shape[0]
    ex_all = examples * T
    both = pj + pk
    cfg = dict(X=X, Z=Z, T=T, Y=Y, NA=NA, NB=NB, TA=TA, CW=CW, TOK=tok)
    NQ = NA + NB
    dma = pltpu.SemaphoreType.DMA
    vmem = pltpu.VMEM
    scratch = [
        vmem(flat_inputs.shape, BF16), vmem(flat_grads.shape, BF16),
        vmem(proj_in.shape, BF16), vmem(proj_out.shape, BF16),
        vmem((min(SLOTS, NB), X, depth, CW // X), F32),
        vmem((NB, X, stored, CW // X), F32),
        vmem((NA, TA, both), F32), vmem((NA, X - 1, TA // X, both), F32),
        vmem((NA, TA // X, both), F32), vmem((NA, 2, TA // X, both), F32),
        vmem((NA, TA, both), F32), vmem((NA, S, pk // S, TA), F32),
        vmem((ex_all, depth), F32), vmem((ex_all, depth), BF16), vmem((ex_all, depth), BF16),
        vmem((NB, X, ex_all, CW // X), F32), vmem((NB, X - 1, ex_all, CW // X), F32),
        vmem((NB, ex_all, CW // X), F32), vmem((NB, 2, ex_all, CW // X), F32),
        vmem((NB, ex_all, CW // X), F32),
        vmem((X, ex_all, stored), F32), vmem((T - 1, X, examples, stored), F32),
        vmem((X, examples, stored), F32), vmem((X - 1, examples, stored), F32),
        dma((NA, 2)), dma((2,)), dma((min(SLOTS, NB), X)), dma((NB,)),
        dma((NQ, X - 1)), dma((NQ, X - 1)), dma((NQ,)), dma((NQ, 2)),
        dma((NQ,)), dma((NQ,)), dma((NA, X - 1)), dma((NA, X - 1)),
        dma((NA, max(Y - 1, 1))), dma((NA, max(Y - 1, 1))), dma((NA, Y)), dma((NA, Y)),
        dma((NB, X - 1)), dma((NB, X - 1)), dma((T - 1,)), dma((T - 1,)),
        dma((X - 1,)), dma((X - 1,)),
    ]
    hbm = pl.BlockSpec(memory_space=pl.ANY)
    return pl.pallas_call(
        functools.partial(kernel, cfg),
        out_shape=jax.ShapeDtypeStruct((examples, stored), F32),
        in_specs=[hbm] * 6,
        out_specs=pl.BlockSpec(memory_space=pltpu.VMEM),
        scratch_shapes=scratch,
        compiler_params=pltpu.CompilerParams(
            collective_id=0, has_side_effects=True, vmem_limit_bytes=60 * 1024 * 1024
        ),
    )(flat_inputs, flat_grads, proj_in, proj_out, inv_fisher, store_grads)


def solution(mesh):
    placed = (
        P("tensor", None, "store"),
        P("tensor", None, "store"),
        P("store", None),
        P("store", None),
        P("store", "tensor"),
        P("store", "tensor"),
    )
    return jax.shard_map(
        functools.partial(on_device, dict(mesh.shape)), mesh=mesh, in_specs=placed,
        out_specs=P("tensor", "store"), check_vma=False,
    )
```
